256 devices in a mesh: ex: 32 (over x, z_lo, core), tp: 8 (over y, z_hi).
Axes of the slice: x: 4, y: 4, z: 8 (z_hi: 2, z_lo: 4; z = z_hi * 4 + z_lo), core: 2. Of those that a mesh axis runs over, the one named last changes fastest.
Arguments:
- acts: bfloat16 [16384, 8192], P('ex', 'tp'), may hold values from -6 to 6
- grads: bfloat16 [16384, 8192], P('ex', 'tp'), may hold values from -6 to 6
- in_basis: bfloat16 [8192, 4096], P('tp', 'ex'), may hold values from -0.0625 to 0.0625
- out_basis: bfloat16 [8192, 4096], P('tp', 'ex'), may hold values from -0.0625 to 0.0625
Outputs:
- correction: float32 [4096, 4096], P('tp', 'ex')
The draws below stay inside these ranges and needn't reach their ends.
All inputs are finite; a program needn't handle non-finite values.
Results may differ from the reference program's by a relative error of at most 0.0055.
Values may be sent and summed in bfloat16 or wider, within the bound.
No kernel may reach another device: no remote copies, remote signals or barrier semaphores. Data moves between devices by JAX's collectives and lax.ppermute only.
A program may use at most 64 MiB of HBM per device.

```python
import jax
import jax.numpy as jnp
from jax import lax

D = 8192
WA = 4096
WG = 4096
SEQ = 256
EXAMPLES = 64
TOKENS = 16384
N_TP = 8


def steps_of(key, shape, shards, least, high):
    level, own = 1.0, jax.random.fold_in(key, 6)
    for dim, blocks in shards:
        heights = jnp.exp(jax.random.uniform(jax.random.fold_in(own, dim), (blocks,), jnp.float32, least / len(shards), high / len(shards)))
        level = level * jnp.repeat(heights, shape[dim] // blocks).reshape([-1 if axis == dim else 1 for axis in range(len(shape))])
    return level


def scatter_about(key, extent, spread, bound, split=(), kind=jnp.bfloat16):
    level = steps_of(key, extent, split, -0.22, 0.18) if split else 1.0
    entries = jax.random.normal(key, extent, jnp.float32) * spread * level
    return jnp.minimum(jnp.maximum(entries, -bound), bound).astype(kind)


def setup_inputs(seed: int = 0) -> dict:
    key_list = jax.random.split(jax.random.key(seed), 5)
    acts = scatter_about(key_list[0], (TOKENS, D), 1.0, 6.0, ((0, 32), (1, 8)))
    grads = scatter_about(key_list[1], (TOKENS, D), 1.0, 6.0, ((0, 32), (1, 8)))
    in_basis = scatter_about(key_list[2], (D, WA), D ** -0.5, 0.0625, ((0, 8), (1, 32)))
    out_basis = scatter_about(key_list[3], (D, WG), D ** -0.5, 0.0625, ((0, 8), (1, 32)))
    return {"acts": acts, "grads": grads, "in_basis": in_basis, "out_basis": out_basis}


def project(data, basis):
    block = D // N_TP
    total = jnp.zeros((data.shape[0], basis.shape[1]), jnp.float32)
    for index in range(N_TP):
        partial_term = jnp.dot(data[:, index * block:(index + 1) * block], basis[index * block:(index + 1) * block, :], preferred_element_type=jnp.float32)
        rounded = lax.optimization_barrier(partial_term.astype(jnp.bfloat16))
        total = total + rounded.astype(jnp.float32)
    return total.astype(jnp.bfloat16)


def reference(acts, grads, in_basis, out_basis):
    in_proj = project(acts, in_basis).reshape(EXAMPLES, SEQ, WA)
    out_proj = project(grads, out_basis).reshape(EXAMPLES, SEQ, WG)

    def step(carry, pair):
        grad_rows, act_rows = pair
        proj_grad = jnp.dot(grad_rows.T, act_rows, preferred_element_type=jnp.float32)
        return carry + proj_grad * proj_grad, None

    start = jnp.zeros((WG, WA), jnp.float32)
    total, unused = lax.scan(step, start, (out_proj, in_proj))
    return total * (1.0 / (EXAMPLES * SEQ))
```

```python
import functools

import jax
import jax.numpy as jnp
from jax import lax
from jax.experimental import pallas as pl
from jax.experimental.pallas import tpu as pltpu
from jax.sharding import PartitionSpec as P

SEQ = 256
NX, NY, NZ_LO, NZ_HI, NC = 4, 4, 4, 2, 2
PHASES = 2
X_TWO_STEP = False
Y_TWO_STEP = False


def position(index):
    ex, tp = divmod(index, NY * NZ_HI)
    x, rest = divmod(ex, NZ_LO * NC)
    z_lo, core = divmod(rest, NC)
    y, z_hi = divmod(tp, NZ_HI)
    return x, y, z_hi, z_lo, core


def number(x, y, z_hi, z_lo, core):
    ex = ((x % NX) * NZ_LO + z_lo) * NC + core
    return ex * NY * NZ_HI + (y % NY) * NZ_HI + z_hi


def move(array, target):
    pairs = []
    for index in range(NX * NY * NZ_LO * NZ_HI * NC):
        goal = target(*position(index))
        if goal is not None:
            pairs.append((index, number(*goal)))
    return lax.ppermute(array, ("ex", "tp"), pairs)


def other_core(x, y, h, l, c):
    return x, y, h, l, 1 - c


def along_x(step):
    return lambda x, y, h, l, c: (x + step, y, h, l, c)


def along_y(step):
    return lambda x, y, h, l, c: (x, y + step, h, l, c)


def other_half(x, y, h, l, c):
    return x, y, 1 - h, l, c


def square_kernel(seqs, block, shift_ref, rows_ref, cols_ref, own_ref, *sent_refs):
    shift = shift_ref[0]
    scale = 1.0 / 16384
    for step, out_ref in enumerate((own_ref, *sent_refs)):
        start = pl.multiple_of(lax.rem(shift + step, NX) * block, block)
        total = None
        for seq in range(seqs):
            tokens = pl.ds(seq * SEQ, SEQ)
            term = lax.dot_general(
                rows_ref[tokens, :],
                cols_ref[tokens, pl.ds(start, block)],
                (((0,), (0,)), ((), ())),
                preferred_element_type=jnp.float32,
            )
            term = term * term
            total = term if total is None else total + term
        out_ref[...] = (total * scale).astype(out_ref.dtype)


def squares(shift, rows, cols):
    tokens, height = rows.shape
    width = cols.shape[1] // NX
    vmem = pl.BlockSpec(memory_space=pltpu.VMEM)
    return pl.pallas_call(
        functools.partial(square_kernel, tokens // SEQ, width),
        out_shape=[jax.ShapeDtypeStruct((height, width), jnp.float32)]
        + [jax.ShapeDtypeStruct((height, width), jnp.bfloat16)] * (NX - 1),
        in_specs=[pl.BlockSpec(memory_space=pltpu.SMEM), vmem, vmem],
        out_specs=[vmem] * NX,
        compiler_params=pltpu.CompilerParams(vmem_limit_bytes=40 * 1024 * 1024),
        cost_estimate=pl.CostEstimate(
            flops=2 * tokens * height * width * NX, bytes_accessed=8 << 20, transcendentals=0
        ),
        name="squares",
    )(shift.reshape(1), rows, cols)


def gather_x(own):
    before = move(own, along_x(1))
    after = move(own, along_x(-1))
    if X_TWO_STEP:
        half = own.shape[0] // 2
        across = jnp.concatenate(
            [move(before[:half], along_x(1)), move(after[half:], along_x(-1))], axis=0
        )
    else:
        across = move(own, along_x(2))
    return own, after, across, before


def scatter_y(terms):
    f32 = lambda value: value.astype(jnp.float32)
    if Y_TWO_STEP:
        half = terms[2].shape[0] // 2
        up = move(terms[2][:half], along_y(1))
        down = move(terms[2][half:], along_y(-1))
        nxt = jnp.concatenate(
            [(f32(terms[1][:half]) + f32(up)).astype(jnp.bfloat16), terms[1][half:]], axis=0
        )
        prv = jnp.concatenate(
            [terms[3][:half], (f32(terms[3][half:]) + f32(down)).astype(jnp.bfloat16)], axis=0
        )
        got = [move(nxt, along_y(1)), move(prv, along_y(-1))]
    else:
        got = [move(terms[1], along_y(1)), move(terms[3], along_y(-1)), move(terms[2], along_y(2))]
    total = f32(terms[0])
    for value in got:
        total = total + f32(value)
    return total


def on_device(acts, grads, in_basis, out_basis):
    ex, tp = lax.axis_index("ex"), lax.axis_index("tp")
    x, z_lo, core = ex // (NZ_LO * NC), ex // NC % NZ_LO, ex % NC
    y, z_hi = tp // NZ_HI, tp % NZ_HI
    first = core == 0
    low = z_hi == 0
    width = in_basis.shape[1]

    with jax.named_scope("to_cores"):
        basis_in = move(jnp.where(first, out_basis, in_basis), other_core)
        own_basis = jnp.concatenate(
            [jnp.where(first, in_basis, basis_in), jnp.where(first, basis_in, out_basis)], axis=1
        )
        data_in = move(jnp.where(first, grads, acts), other_core)
        data = jnp.concatenate(
            [jnp.where(first, acts, data_in), jnp.where(first, data_in, grads)], axis=0
        )

    with jax.named_scope("basis_along_z"):
        chunks = [own_basis] + [
            move(own_basis, lambda x, y, h, l, c, k=k: (x, y, h, l ^ k, c)) for k in range(1, NZ_LO)
        ]

    per = NZ_LO // PHASES
    in_parts, out_parts = [], []
    for phase in range(PHASES):
        own = jnp.concatenate(chunks[phase * per : (phase + 1) * per], axis=1)
        with jax.named_scope("basis_along_x"):
            bases = jnp.stack(gather_x(own))
        with jax.named_scope("project"):
            terms = []
            for step in range(NY):
                basis = lax.dynamic_index_in_dim(bases, (y + step - x) % NX, 0, keepdims=False)
                term = jnp.dot(data, basis, preferred_element_type=jnp.float32)
                terms.append(term.astype(jnp.bfloat16))
        with jax.named_scope("sum_along_y"):
            partial = scatter_y(terms)
        with jax.named_scope("sum_z_halves"):
            halves = partial.reshape(partial.shape[0], per, NC, width)
            kept = jnp.where(low, halves[:, :, 0], halves[:, :, 1])
            sent = jnp.where(low, halves[:, :, 1], halves[:, :, 0])
            sent = sent.reshape(partial.shape[0], per * width).astype(jnp.bfloat16)
            kept = kept.reshape(partial.shape[0], per * width)
            proj = (kept + move(sent, other_half).astype(jnp.float32)).astype(jnp.bfloat16)
        with jax.named_scope("gather"):
            prev = move(
                proj,
                lambda x, y, h, l, c: (x, y + 1, h, l, c) if c == 0 else (x, y, 1 - h, l, c),
            )
            nxt = move(proj, lambda x, y, h, l, c: (x, y - 1, h, l, c) if c == 0 else None)
            across = move(proj, lambda x, y, h, l, c: (x, y + 2, h, l, c) if c == 0 else None)
            for k in range(per):
                cut = slice(k * width, (k + 1) * width)
                in_parts.append([part[:, cut] for part in (proj, nxt, across, prev)])
                a, b = proj[:, cut], prev[:, cut]
                out_parts.append([jnp.where(low, a, b), jnp.where(low, b, a)])

    with jax.named_scope("between_cores"):
        half = NZ_LO // 2
        out_all = jnp.concatenate([part for pair in out_parts for part in pair], axis=1)
        in_low, in_high = (
            jnp.concatenate(
                [in_parts[k][step] for step in range(NY) for k in range(at, at + half)], axis=1
            )
            for at in (0, half)
        )
        got = move(jnp.where(first, in_high, out_all), other_core)
        rows = jnp.where(first, got, out_all)
        cols = jnp.where(first, in_low, got)

    with jax.named_scope("squares"):
        own, *sent = squares((x - y + NY) % NY, rows, cols)

    with jax.named_scope("sum_along_x"):
        total = own
        for step, value in enumerate(sent, 1):
            total = total + move(value, along_x(step)).astype(jnp.float32)
        total = total.astype(jnp.bfloat16)

    with jax.named_scope("sum_along_z"):
        height = total.shape[0] // 2
        result = jnp.zeros((height, width), jnp.float32)
        for a in range(2):
            for b in range(2):
                got = move(
                    total[a * height : (a + 1) * height, b * width : (b + 1) * width],
                    lambda x, y, h, l, c, a=a, b=b: (x, y, a ^ (l >> 1), l ^ (2 * c + b), h),
                ).astype(jnp.float32)
                turned = jnp.concatenate([got[height // 2 :], got[: height // 2]], axis=0)
                result = result + jnp.where(z_lo % 2 == b, got, turned)
    return result


def solution(mesh):
    return jax.shard_map(
        on_device,
        mesh=mesh,
        in_specs=(P("ex", "tp"), P("ex", "tp"), P("tp", "ex"), P("tp", "ex")),
        out_specs=P("tp", "ex"),
        check_vma=False,
    )
```

```python
import functools

import jax
import jax.numpy as jnp
from jax import lax
from jax.experimental import pallas as pl
from jax.experimental.pallas import tpu as pltpu
from jax.sharding import PartitionSpec as P

SEQ = 256
NX, NY, NZ_LO, NZ_HI, NC = 4, 4, 4, 2, 2
X_MODE = "two"
Y_MODE = "two"
FAR_SWAP = True
PHASES = ((0,), (1,), (2,), (3,))
GROUPS = ((0, 1), (2, 3))
AFTER = {
    "X2.0": ("Z1",),
    "X1.1": ("X2.0",),
    "X2.1": ("Y1.0", "Z2"),
    "X1.2": ("X2.1",),
    "X2.2": ("Z3", "Y1.1", "Y2.0"),
    "X1.3": ("X2.2", "H.0"),
    "X2.3": ("Y1.2", "Y2.1"),
    "Y2.3": ("H.1", "Y2.2"),
    "H.3": ("G.1",),
}


def position(index):
    ex, tp = divmod(index, NY * NZ_HI)
    x, rest = divmod(ex, NZ_LO * NC)
    z_lo, core = divmod(rest, NC)
    y, z_hi = divmod(tp, NZ_HI)
    return x, y, z_hi, z_lo, core


def number(x, y, z_hi, z_lo, core):
    ex = ((x % NX) * NZ_LO + z_lo) * NC + core
    return ex * NY * NZ_HI + (y % NY) * NZ_HI + z_hi


def move(array, target):
    pairs = []
    for index in range(NX * NY * NZ_LO * NZ_HI * NC):
        goal = target(*position(index))
        if goal is not None:
            pairs.append((index, number(*goal)))
    return lax.ppermute(array, ("ex", "tp"), pairs)


def other_core(x, y, h, l, c):
    return x, y, h, l, 1 - c


def along_x(step):
    return lambda x, y, h, l, c: (x + step, y, h, l, c)


def along_y(step):
    return lambda x, y, h, l, c: (x, y + step, h, l, c)


def other_half(x, y, h, l, c):
    return x, y, 1 - h, l, c


def square_kernel(seqs, block, start_ref, rows_ref, cols_ref, *out_refs):
    scale = 1.0 / 16384
    for index, out_ref in enumerate(out_refs):
        start = pl.multiple_of(start_ref[index] * block, block)
        total = None
        for seq in range(seqs):
            tokens = pl.ds(seq * SEQ, SEQ)
            term = lax.dot_general(
                rows_ref[tokens, :],
                cols_ref[tokens, pl.ds(start, block)],
                (((0,), (0,)), ((), ())),
                preferred_element_type=jnp.float32,
            )
            term = term * term
            total = term if total is None else total + term
        out_ref[...] = (total * scale).astype(out_ref.dtype)


def squares(starts, rows, cols):
    tokens, height = rows.shape
    width = cols.shape[1] // 4
    vmem = pl.BlockSpec(memory_space=pltpu.VMEM)
    return pl.pallas_call(
        functools.partial(square_kernel, tokens // SEQ, width),
        out_shape=[jax.ShapeDtypeStruct((height, width), jnp.bfloat16)] * 4,
        in_specs=[pl.BlockSpec(memory_space=pltpu.SMEM), vmem, vmem],
        out_specs=[vmem] * 4,
        compiler_params=pltpu.CompilerParams(vmem_limit_bytes=40 * 1024 * 1024),
        cost_estimate=pl.CostEstimate(
            flops=2 * tokens * height * width * 4, bytes_accessed=8 << 20, transcendentals=0
        ),
        name="squares",
    )(starts, rows, cols)


def f32(value):
    return value.astype(jnp.float32)


def bf16(value):
    return value.astype(jnp.bfloat16)


def gather_x(order, phase, own):
    before = move(own, along_x(1))
    behind = move(own, along_x(-1))
    if X_MODE == "direct":
        across = move(own, along_x(2))
        return jnp.stack([own, behind, across, before])
    half = own.shape[0] // 2
    before, behind = order.mark(f"X1.{phase}", before, behind)
    left, right = order.wait(f"X2.{phase}", before[:half], behind[half:])
    across = jnp.concatenate([move(left, along_x(1)), move(right, along_x(-1))], axis=0)
    return jnp.stack([own, behind, across, before])


def scatter_y(order, phase, term):
    two = bf16(term(2))
    half = two.shape[0] // 2
    if Y_MODE == "direct":
        one, three, own = (bf16(term(step)) for step in (1, 3, 0))
        got = [move(two, along_y(2)), move(one, along_y(1)), move(three, along_y(-1))]
    else:
        up, down = move(two[:half], along_y(1)), move(two[half:], along_y(-1))
        one, three, own = (bf16(term(step)) for step in (1, 3, 0))
        up, down = order.mark(f"Y1.{phase}", up, down)
        up, down = order.wait(f"Y2.{phase}", up, down)
        nxt = jnp.concatenate([bf16(f32(one[:half]) + f32(up)), one[half:]], axis=0)
        prv = jnp.concatenate([three[:half], bf16(f32(three[half:]) + f32(down))], axis=0)
        got = [move(nxt, along_y(1)), move(prv, along_y(-1))]
    total = f32(own)
    for value in got:
        total = total + f32(value)
    return total


class Order:
    def __init__(self):
        self.done = {}

    def mark(self, name, *values):
        self.done[name] = values[0]
        return values

    def wait(self, name, *values):
        others = [self.done[other] for other in AFTER.get(name, ()) if other in self.done]
        if not others:
            return values
        return lax.optimization_barrier((*values, *others))[: len(values)]


def on_device(acts, grads, in_basis, out_basis):
    ex, tp = lax.axis_index("ex"), lax.axis_index("tp")
    x, z_lo, core = ex // (NZ_LO * NC), ex // NC % NZ_LO, ex % NC
    y, z_hi = tp // NZ_HI, tp % NZ_HI
    first = core == 0
    low = z_hi == 0
    width = in_basis.shape[1]

    with jax.named_scope("to_cores"):
        basis_in = move(jnp.where(first, out_basis, in_basis), other_core)
        own_basis = jnp.concatenate(
            [jnp.where(first, in_basis, basis_in), jnp.where(first, basis_in, out_basis)], axis=1
        )
        data_in = move(jnp.where(first, grads, acts), other_core)
        data = jnp.concatenate(
            [jnp.where(first, acts, data_in), jnp.where(first, data_in, grads)], axis=0
        )

    order = Order()
    with jax.named_scope("basis_along_z"):
        chunks = [own_basis]
        for k in range(1, NZ_LO):
            chunks += order.mark(
                f"Z{k}", move(own_basis, lambda x, y, h, l, c, k=k: (x, y, h, l ^ k, c))
            )

    own_cols, far_cols, own_rows, far_rows, projs = [], [], [], [], []
    for phase, members in enumerate(PHASES):
        with jax.named_scope("basis_along_x"):
            chunk = jnp.concatenate([chunks[k] for k in members], axis=1)
            (chunk,) = order.wait(f"X1.{phase}", chunk)
            bases = gather_x(order, phase, chunk)
            (bases,) = order.mark(f"X2.{phase}", bases)
        with jax.named_scope("project"):
            (ready,) = order.wait(f"D.{phase}", data)

            def term(step):
                at = (y + step - x + NX) % NX
                basis = lax.dynamic_index_in_dim(bases, at, 0, keepdims=False)
                return jnp.dot(ready, basis, preferred_element_type=jnp.float32)

        with jax.named_scope("sum_along_y"):
            partial = scatter_y(order, phase, term)
        with jax.named_scope("sum_z_halves"):
            cuts = [partial[:, k * width : (k + 1) * width] for k in range(NC * len(members))]
            even, odd = jnp.concatenate(cuts[::2], axis=1), jnp.concatenate(cuts[1::2], axis=1)
            sent = bf16(jnp.where(low, odd, even))
            (sent,) = order.mark(f"Y2.{phase}", sent)
            (sent,) = order.wait(f"H.{phase}", sent)
            proj = bf16(jnp.where(low, even, odd) + f32(move(sent, other_half)))
            (proj,) = order.mark(f"H.{phase}", proj)
            projs.append(proj)
        group = next(group for group in GROUPS if phase in group)
        if phase != group[-1]:
            continue
        with jax.named_scope("gather"):
            proj = jnp.concatenate(projs[group[0] : group[-1] + 1], axis=1)
            prev = move(
                proj,
                lambda x, y, h, l, c: (x, y + 1, h, l, 1) if c == 0 else (x, y, 1 - h, l, 0),
            )
            nxt = move(proj, lambda x, y, h, l, c: (x, y - 1, h, l, 1) if c == 0 else (x, y, h, l, 0))
            if FAR_SWAP:
                across = move(proj, lambda x, y, h, l, c: (x, y + 2, h, l, 0) if c == 0 else None)
                far = move(prev, lambda x, y, h, l, c: (x, y, h, l, 1) if c == 0 else None)
            else:
                across = far = move(
                    proj,
                    lambda x, y, h, l, c: (x, y + 2, h, l, 0) if c == 0 else (x, y, 1 - h, l, 1),
                )
            own_cols.append(jnp.where(first, proj, nxt))
            far_cols.append(jnp.where(first, across, prev))
            own_rows.append(jnp.where(first, nxt, proj))
            far_rows.append(jnp.where(first, prev, far))
            order.mark(f"G.{phase}", own_cols[-1])

    with jax.named_scope("squares"):
        a, b = jnp.concatenate(own_rows, axis=1), jnp.concatenate(far_rows, axis=1)
        rows = jnp.concatenate(
            [
                part[:, k * width : (k + 1) * width]
                for k in range(NZ_LO)
                for part in (jnp.where(low, a, b), jnp.where(low, b, a))
            ],
            axis=1,
        )
        cols = jnp.concatenate(own_cols + far_cols, axis=1)
        steps = (y + core - x + NX) % NX
        odd, turn = steps % 2, steps // 2
        starts = jnp.stack([2 * (d ^ turn) + (goal ^ odd) for d in range(2) for goal in range(2)])
        tiles = squares(starts, rows, cols)

    with jax.named_scope("sum_along_x"):
        total = None
        for d in range(2):
            for goal in range(2):

                def target(x, y, h, l, c, d=d, goal=goal):
                    odd = (y + c - x) % 2
                    return x + odd + 2 * d, y, h, l, goal ^ odd

                value = f32(move(tiles[2 * d + goal], target))
                total = value if total is None else total + value
        total = bf16(total)

    with jax.named_scope("sum_along_z"):
        height = total.shape[0] // 2
        result = jnp.zeros((height, width), jnp.float32)
        for a in range(2):
            for b in range(2):
                got = move(
                    total[a * height : (a + 1) * height, b * width : (b + 1) * width],
                    lambda x, y, h, l, c, a=a, b=b: (x, y, a ^ (l >> 1), l ^ (2 * c + b), h),
                ).astype(jnp.float32)
                turned = jnp.concatenate([got[height // 2 :], got[: height // 2]], axis=0)
                result = result + jnp.where(z_lo % 2 == b, got, turned)
    return result


def solution(mesh):
    return jax.shard_map(
        on_device,
        mesh=mesh,
        in_specs=(P("ex", "tp"), P("ex", "tp"), P("tp", "ex"), P("tp", "ex")),
        out_specs=P("tp", "ex"),
        check_vma=False,
    )
```

```python
import functools

import jax
import jax.numpy as jnp
from jax import lax
from jax.experimental import pallas as pl
from jax.experimental.pallas import tpu as pltpu
from jax.sharding import PartitionSpec as P

SEQ = 256
NX, NY, NZ_LO, NZ_HI, NC = 4, 4, 4, 2, 2
EARLY = (1, 2)
GROUPS = ((0, 1), (2, 3))
ORDER = (
    "far0", "near1", "two0", "rest0", "zed3", "far1", "near2", "sum0", "two1", "rest1", "far2",
    "near3", "half0", "sum1", "two2", "rest2", "far3", "sum2", "half1", "two3", "rest3", "proj0",
    "sum3", "late2", "proj1", "send0", "late3", "full2", "full3", "push1", "keep0", "hold1",
)


def position(index):
    ex, tp = divmod(index, NY * NZ_HI)
    x, rest = divmod(ex, NZ_LO * NC)
    z_lo, core = divmod(rest, NC)
    y, z_hi = divmod(tp, NZ_HI)
    return x, y, z_hi, z_lo, core


def number(x, y, z_hi, z_lo, core):
    ex = ((x % NX) * NZ_LO + z_lo) * NC + core
    return ex * NY * NZ_HI + (y % NY) * NZ_HI + z_hi


def move(array, target):
    pairs = []
    for index in range(NX * NY * NZ_LO * NZ_HI * NC):
        goal = target(*position(index))
        if goal is not None:
            pairs.append((index, number(*goal)))
    return lax.ppermute(array, ("ex", "tp"), pairs)


def other_core(x, y, h, l, c):
    return x, y, h, l, 1 - c


def along_x(step):
    return lambda x, y, h, l, c: (x + step, y, h, l, c)


def along_y(step):
    return lambda x, y, h, l, c: (x, y + step, h, l, c)


def by_core_x(x, y, h, l, c):
    return x + 1 - 2 * c, y, h, l, c


def by_core_y(x, y, h, l, c):
    return x, y + 1 - 2 * c, h, l, c


def other_half(x, y, h, l, c):
    return x, y, 1 - h, l, c


def f32(value):
    return value.astype(jnp.float32)


def bf16(value):
    return value.astype(jnp.bfloat16)


def like(shape, dtype=jnp.bfloat16):
    return jax.ShapeDtypeStruct(shape, dtype)


def pick(out_ref, refs, index):
    for at, ref in enumerate(refs):

        @pl.when(index == at)
        def _(ref=ref):
            out_ref[...] = ref[...]


def copy_body(scalars, ins, outs, scratch):
    for in_ref, out_ref in zip(ins, outs):
        out_ref[...] = in_ref[...]


def far_body(scalars, ins, outs, scratch):
    pick(outs[0], ins, 1 - scalars[1])


def project_body(steps, scalars, ins, outs, scratch):
    data, *pieces = ins
    (basis,) = scratch
    for step, out_ref in zip(steps, outs):
        pick(basis, pieces, lax.rem(scalars[0] + step, NX))
        out_ref[...] = bf16(jnp.dot(data[...], basis[...], preferred_element_type=jnp.float32))


def sum_body(scalars, ins, outs, scratch):
    one, three, got = ins
    nxt, prv = outs

    @pl.when(scalars[1] == 1)
    def _():
        nxt[...] = bf16(f32(one[...]) + f32(got[...]))
        prv[...] = three[...]

    @pl.when(scalars[1] == 0)
    def _():
        nxt[...] = one[...]
        prv[...] = bf16(f32(three[...]) + f32(got[...]))


def half_body(scalars, ins, outs, scratch):
    sent, kept = outs
    width = sent.shape[1]
    for low, (keep, send) in ((1, (0, width)), (0, (width, 0))):

        @pl.when(scalars[2] == low)
        def _(keep=keep, send=send):
            sent[...] = bf16(sum(f32(ref[:, send : send + width]) for ref in ins))
            kept[...] = sum(f32(ref[:, keep : keep + width]) for ref in ins)


def late_body(scalars, ins, outs, scratch):
    total_ref, away, kept = outs
    width = away.shape[1]
    total = sum(f32(ref[...]) for ref in ins)
    total_ref[...] = total
    for low, (keep, send) in ((1, (0, width)), (0, (width, 0))):

        @pl.when(scalars[2] == low)
        def _(keep=keep, send=send):
            away[...] = bf16(total[:, send : send + width])
            kept[...] = bf16(total[:, keep : keep + width])


def full_body(scalars, ins, outs, scratch):
    total, mine, theirs = ins
    (out,) = outs
    width = mine.shape[1]
    for first in (1, 0):
        for low in (1, 0):

            @pl.when((scalars[1] == first) & (scalars[2] == low))
            def _(first=first, low=low):
                own = (1 - low) * width
                other = low * width
                at = 0 if first else own
                out[:, at : at + width] = bf16(total[:, own : own + width] + f32(mine[...]))
                if first:
                    out[:, width:] = jnp.zeros(mine.shape, jnp.bfloat16)
                else:
                    out[:, other : other + width] = bf16(
                        total[:, other : other + width] + f32(theirs[...])
                    )


def send_late_body(scalars, ins, outs, scratch):
    width = ins[0].shape[1] // 2

    @pl.when(scalars[1] == 1)
    def _():
        for out_ref in outs:
            for at, ref in enumerate(ins):
                out_ref[:, at * width : (at + 1) * width] = ref[:, :width]

    @pl.when(scalars[1] == 0)
    def _():
        for index in range(2 * len(ins)):
            out_ref, at = outs[index // len(ins)], index % len(ins)
            start = index % 2 * width
            out_ref[:, at * width : (at + 1) * width] = ins[index // 2][:, start : start + width]


def keep_late_body(scalars, ins, outs, scratch):
    one, two, prev, nxt, across = ins
    rows, own_cols, far_cols = outs
    width = one.shape[1]
    for first, (left, right, own, far) in ((1, (prev, nxt, one, across)), (0, (one, two, nxt, prev))):

        @pl.when(scalars[1] == first)
        def _(left=left, right=right, own=own, far=far):
            rows[:, :width] = left[...]
            rows[:, width:] = right[...]
            own_cols[...] = own[...]
            far_cols[...] = far[...]


def proj_body(scalars, ins, outs, scratch):
    outs[0][...] = bf16(ins[0][...] + f32(ins[1][...]))


def join_body(scalars, ins, outs, scratch):
    width = ins[0].shape[1]
    for at, ref in enumerate(ins):
        outs[0][:, at * width : (at + 1) * width] = ref[...]


def keep_body(width, scalars, ins, outs, scratch):
    proj, prev, nxt, across, far = ins
    rows, own_cols, far_cols = outs
    for first, (own, other, mine, theirs) in (
        (1, (proj, across, nxt, prev)),
        (0, (nxt, prev, proj, far)),
    ):

        @pl.when(scalars[1] == first)
        def _(own=own, other=other):
            own_cols[...] = own[...]
            far_cols[...] = other[...]

        for low, pair in ((1, (mine, theirs)), (0, (theirs, mine))):

            @pl.when((scalars[1] == first) & (scalars[2] == low))
            def _(pair=pair):
                for k in range(own_cols.shape[1] // width):
                    for at, ref in enumerate(pair):
                        start = (2 * k + at) * width
                        rows[:, start : start + width] = ref[:, k * width : (k + 1) * width]


def square_body(places, scalars, ins, outs, scratch):
    (cols,) = scratch
    rows = ins[: len(GROUPS)]
    for index, out_ref in enumerate(outs):
        for block, parts in enumerate(places):

            @pl.when(scalars[3 + index] == block)
            def _(parts=parts):
                width = cols.shape[1] // len(parts)
                for at, (which, start) in enumerate(parts):
                    cols[:, at * width : (at + 1) * width] = ins[which][:, start : start + width]

        start = 0
        for ref in rows:
            total = None
            for seq in range(ref.shape[0] // SEQ):
                tokens = pl.ds(seq * SEQ, SEQ)
                term = lax.dot_general(
                    ref[tokens, :],
                    cols[tokens, :],
                    (((0,), (0,)), ((), ())),
                    preferred_element_type=jnp.float32,
                )
                total = term * term if total is None else total + term * term
            out_ref[start : start + ref.shape[1], :] = bf16(total * (1.0 / 16384))
            start += ref.shape[1]


def cut_body(scalars, ins, outs, scratch):
    total = sum(f32(ref[...]) for ref in ins)
    height, width = outs[0].shape
    for index, out_ref in enumerate(outs):
        a, b = divmod(index, 2)
        out_ref[...] = bf16(total[a * height : (a + 1) * height, b * width : (b + 1) * width])


def last_body(scalars, ins, outs, scratch):
    half = outs[0].shape[0] // 2
    for odd in range(2):

        @pl.when(scalars[7] == odd)
        def _(odd=odd):
            for at in (0, half):
                total = None
                for index, ref in enumerate(ins):
                    start = at if index % 2 == odd else half - at
                    term = f32(ref[start : start + half, :])
                    total = term if total is None else total + term
                outs[0][at : at + half, :] = total


class Chain:
    def __init__(self, scalars):
        self.scalars = scalars
        self.token = jnp.zeros((8, 128), jnp.float32)

    def __call__(self, name, body, ins, outs, scratch=()):
        def kernel(scalars, token, *refs):
            in_refs, refs = refs[: len(ins)], refs[len(ins) :]
            out_refs, token_out, scratch_refs = refs[: len(outs)], refs[len(outs)], refs[len(outs) + 1 :]
            body(scalars, in_refs, out_refs, scratch_refs)
            token_out[...] = token[...]

        vmem = pl.BlockSpec(memory_space=pltpu.VMEM)
        *results, self.token = pl.pallas_call(
            kernel,
            out_shape=[*outs, like((8, 128), jnp.float32)],
            in_specs=[pl.BlockSpec(memory_space=pltpu.SMEM)] + [vmem] * (1 + len(ins)),
            out_specs=[vmem] * (len(outs) + 1),
            scratch_shapes=list(scratch),
            compiler_params=pltpu.CompilerParams(vmem_limit_bytes=VMEM_LIMIT),
            cost_estimate=pl.CostEstimate(flops=1, bytes_accessed=1, transcendentals=0),
            name=name,
        )(self.scalars, self.token, *ins)
        return results


VMEM_LIMIT = 16 * 1024 * 1024


def on_device(acts, grads, in_basis, out_basis):
    ex, tp = lax.axis_index("ex"), lax.axis_index("tp")
    x, z_lo, core = ex // (NZ_LO * NC), ex // NC % NZ_LO, ex % NC
    y, z_hi = tp // NZ_HI, tp % NZ_HI
    first = core == 0
    width = in_basis.shape[1]

    steps = (y + core - x + NX) % NX
    odd, turn = steps % 2, steps // 2
    blocks = [2 * (d ^ turn) + (goal ^ odd) for d in range(2) for goal in range(2)]
    scalars = jnp.stack([(y - x + NX) % NX, 1 - core, 1 - z_hi, *blocks, z_lo % 2])
    chain = Chain(scalars)

    with jax.named_scope("to_cores"):
        basis_in = move(jnp.where(first, out_basis, in_basis), other_core)
        own_basis = jnp.concatenate(
            [jnp.where(first, in_basis, basis_in), jnp.where(first, basis_in, out_basis)], axis=1
        )
        data_in = move(jnp.where(first, grads, acts), other_core)
        data = jnp.concatenate(
            [jnp.where(first, acts, data_in), jnp.where(first, data_in, grads)], axis=0
        )
    tokens, depth, double = data.shape[0], data.shape[1], own_basis.shape[1]
    near_of, far_of, zed_of, terms_of, half_of = {}, {}, {}, {}, {}
    sums_of, proj_of, sent_of, rows_of, cols_of = {}, {}, {}, {}, {}

    def zed(k, gated=True):
        own = chain("zed", copy_body, [own_basis], [like(own_basis.shape)])[0] if gated else own_basis
        zed_of[k] = move(own, lambda x, y, h, l, c: (x, y, h, l ^ k, c))

    def near(phase):
        own = own_basis
        if phase:
            (own,) = chain("near", copy_body, [zed_of[phase]], [like(own_basis.shape)])
        near_of[phase] = own, move(own, along_x(-1)), move(own, along_x(1))

    def far(phase):
        _, behind, before = near_of[phase]
        (own,) = chain("far", far_body, [before, behind], [like(own_basis.shape)])
        far_of[phase] = move(own, by_core_x)

    def project(phase, steps):
        own, behind, before = near_of[phase]
        return chain(
            "project",
            functools.partial(project_body, steps),
            [data, own, behind, far_of[phase], before],
            [like((tokens, double))] * len(steps),
            [pltpu.VMEM((depth, double), jnp.bfloat16)],
        )

    def two(phase):
        (term,) = project(phase, (2,))
        terms_of[phase] = [move(term, by_core_y)]

    def rest(phase):
        terms_of[phase] += project(phase, (1, 3, 0))

    def sums(phase):
        got, one, three, own = terms_of[phase]
        nxt, prv = chain("sums", sum_body, [one, three, got], [like((tokens, double))] * 2)
        sums_of[phase] = own, move(nxt, along_y(1)), move(prv, along_y(-1))

    def half(phase):
        shape = tokens, width
        sent, kept = chain("half", half_body, sums_of[phase], [like(shape), like(shape, jnp.float32)])
        half_of[phase] = kept, move(sent, other_half)

    def proj(phase):
        (proj_of[phase],) = chain("proj", proj_body, half_of[phase], [like((tokens, width))])

    def send(group):
        own = [proj_of[phase] for phase in GROUPS[group]]
        (own,) = chain("send", join_body, own, [like((tokens, width * len(own)))])
        prev = move(own, lambda x, y, h, l, c: (x, y + 1, h, l, 1) if c == 0 else (x, y, 1 - h, l, 0))
        nxt = move(own, lambda x, y, h, l, c: (x, y - 1, h, l, 1) if c == 0 else (x, y, h, l, 0))
        across = move(own, lambda x, y, h, l, c: (x, y + 2, h, l, 0) if c == 0 else None)
        swapped = move(prev, lambda x, y, h, l, c: (x, y, h, l, 1) if c == 0 else None)
        sent_of[group] = own, prev, nxt, across, swapped

    def keep(group):
        shape = sent_of[group][0].shape
        rows_of[group], *cols_of[group] = chain(
            "keep",
            functools.partial(keep_body, width),
            sent_of[group],
            [like((tokens, 2 * shape[1])), like(shape), like(shape)],
        )

    def late(phase):
        total, away, kept = chain(
            "late",
            late_body,
            sums_of[phase],
            [like((tokens, double), jnp.float32)] + [like((tokens, width))] * 2,
        )
        mine = move(away, other_half)
        theirs = move(kept, lambda x, y, h, l, c: (x, y, 1 - h, l, c) if c else None)
        half_of[phase] = total, mine, theirs

    def full(phase):
        (proj_of[phase],) = chain("full", full_body, half_of[phase], [like((tokens, double))])

    def push(group):
        one, two = chain(
            "push",
            send_late_body,
            [proj_of[phase] for phase in GROUPS[group]],
            [like((tokens, width * len(GROUPS[group])))] * 2,
        )
        prev = move(one, lambda x, y, h, l, c: (x, y + 1, h, l, 1) if c == 0 else (x, y, h, l, 0))
        nxt = move(two, lambda x, y, h, l, c: (x, y - 1, h, l, 1) if c == 0 else (x, y, h, l, 0))
        across = move(one, lambda x, y, h, l, c: (x, y + 2, h, l, 0) if c == 0 else None)
        sent_of[group] = one, two, prev, nxt, across

    def hold(group):
        shape = sent_of[group][0].shape
        rows_of[group], *cols_of[group] = chain(
            "hold", keep_late_body, sent_of[group], [like((tokens, 2 * shape[1])), like(shape), like(shape)]
        )

    run = dict(
        late=late, full=full, push=push, hold=hold,
        zed=zed, near=near, far=far, two=two, rest=rest, sum=sums, half=half, proj=proj, send=send, keep=keep
    )
    near(0)
    for k in EARLY:
        zed(k, gated=False)
    for item in ORDER:
        with jax.named_scope(item[:-1]):
            run[item[:-1]](int(item[-1]))

    height = NZ_LO * width
    with jax.named_scope("squares"):
        rows = [rows_of[group] for group in range(len(GROUPS))]
        cols = [cols for group in range(len(GROUPS)) for cols in cols_of[group]]
        places = []
        for block in range(2):
            for part in range(2):
                found = []
                for k in (2 * part, 2 * part + 1):
                    group = next(at for at, members in enumerate(GROUPS) if k in members)
                    found.append((len(rows) + 2 * group + block, GROUPS[group].index(k) * width))
                places.append(found)
        tiles = chain(
            "squares",
            functools.partial(square_body, places),
            rows + cols,
            [like((2 * height, double))] * 4,
            [pltpu.VMEM((tokens, double), jnp.bfloat16)],
        )
    with jax.named_scope("sum_along_x"):
        arrived = []
        for d in (1, 0):
            for goal in range(2):

                def target(x, y, h, l, c, d=d, goal=goal):
                    odd = (y + c - x) % 2
                    return x + odd + 2 * d, y, h, l, goal ^ odd

                arrived.append(move(tiles[2 * d + goal], target))
        parts = chain("cut", cut_body, arrived, [like((height, width))] * 4)
    with jax.named_scope("sum_along_z"):
        got = [
            move(
                parts[2 * a + b],
                lambda x, y, h, l, c, a=a, b=b: (x, y, a ^ (l >> 1), l ^ (2 * c + b), h),
            )
            for a in range(2)
            for b in range(2)
        ]
        (result,) = chain("last", last_body, got, [like((height, width), jnp.float32)])
    return result


def solution(mesh):
    return jax.shard_map(
        on_device,
        mesh=mesh,
        in_specs=(P("ex", "tp"), P("ex", "tp"), P("tp", "ex"), P("tp", "ex")),
        out_specs=P("tp", "ex"),
        check_vma=False,
    )
```

```python
import functools

import jax
import jax.numpy as jnp
from jax import lax
from jax.experimental import pallas as pl
from jax.experimental.pallas import tpu as pltpu
from jax.sharding import PartitionSpec as P

SEQ = 256
NX, NY, NZ_LO, NZ_HI, NC = 4, 4, 4, 2, 2
EARLY = (1, 2)
GROUPS = ((0, 1), (2, 3))
ORDER = (
    "far0", "near1", "two0", "rest0", "zed3", "far1", "near2", "sum0", "two1", "rest1", "far2",
    "near3", "half0", "sum1", "two2", "rest2", "far3", "sum2", "half1", "two3", "rest3", "proj0",
    "sum3", "late2", "proj1", "send0", "late3", "take0", "full2", "full3", "push1", "keep0",
    "hold1",
)


def position(index):
    ex, tp = divmod(index, NY * NZ_HI)
    x, rest = divmod(ex, NZ_LO * NC)
    z_lo, core = divmod(rest, NC)
    y, z_hi = divmod(tp, NZ_HI)
    return x, y, z_hi, z_lo, core


def number(x, y, z_hi, z_lo, core):
    ex = ((x % NX) * NZ_LO + z_lo) * NC + core
    return ex * NY * NZ_HI + (y % NY) * NZ_HI + z_hi


def move(array, target):
    pairs = []
    for index in range(NX * NY * NZ_LO * NZ_HI * NC):
        goal = target(*position(index))
        if goal is not None:
            pairs.append((index, number(*goal)))
    return lax.ppermute(array, ("ex", "tp"), pairs)


def other_core(x, y, h, l, c):
    return x, y, h, l, 1 - c


def along_x(step):
    return lambda x, y, h, l, c: (x + step, y, h, l, c)


def along_y(step):
    return lambda x, y, h, l, c: (x, y + step, h, l, c)


def by_core_x(x, y, h, l, c):
    return x + 1 - 2 * c, y, h, l, c


def by_core_y(x, y, h, l, c):
    return x, y + 1 - 2 * c, h, l, c


def other_half(x, y, h, l, c):
    return x, y, 1 - h, l, c


def f32(value):
    return value.astype(jnp.float32)


def bf16(value):
    return value.astype(jnp.bfloat16)


def like(shape, dtype=jnp.bfloat16):
    return jax.ShapeDtypeStruct(shape, dtype)


def pick(out_ref, refs, index):
    for at, ref in enumerate(refs):

        @pl.when(index == at)
        def _(ref=ref):
            out_ref[...] = ref[...]


def copy_body(scalars, ins, outs, scratch):
    for in_ref, out_ref in zip(ins, outs):
        out_ref[...] = in_ref[...]


def far_body(scalars, ins, outs, scratch):
    pick(outs[0], ins, 1 - scalars[1])


def project_body(steps, scalars, ins, outs, scratch):
    data, *pieces = ins
    (basis,) = scratch
    for step, out_ref in zip(steps, outs):
        pick(basis, pieces, lax.rem(scalars[0] + step, NX))
        out_ref[...] = bf16(jnp.dot(data[...], basis[...], preferred_element_type=jnp.float32))


def sum_body(scalars, ins, outs, scratch):
    one, three, got = ins
    nxt, prv = outs

    @pl.when(scalars[1] == 1)
    def _():
        nxt[...] = bf16(f32(one[...]) + f32(got[...]))
        prv[...] = three[...]

    @pl.when(scalars[1] == 0)
    def _():
        nxt[...] = one[...]
        prv[...] = bf16(f32(three[...]) + f32(got[...]))


def half_body(scalars, ins, outs, scratch):
    sent, kept = outs
    width = sent.shape[1]
    for low, (keep, send) in ((1, (0, width)), (0, (width, 0))):

        @pl.when(scalars[2] == low)
        def _(keep=keep, send=send):
            sent[...] = bf16(sum(f32(ref[:, send : send + width]) for ref in ins))
            kept[...] = sum(f32(ref[:, keep : keep + width]) for ref in ins)


def late_body(scalars, ins, outs, scratch):
    total_ref, away, kept = outs
    width = away.shape[1]
    total = sum(f32(ref[...]) for ref in ins)
    total_ref[...] = total
    for low, (keep, send) in ((1, (0, width)), (0, (width, 0))):

        @pl.when(scalars[2] == low)
        def _(keep=keep, send=send):
            away[...] = bf16(total[:, send : send + width])
            kept[...] = bf16(total[:, keep : keep + width])


def full_body(scalars, ins, outs, scratch):
    total, mine, theirs = ins
    (out,) = outs
    width = mine.shape[1]
    for first in (1, 0):
        for low in (1, 0):

            @pl.when((scalars[1] == first) & (scalars[2] == low))
            def _(first=first, low=low):
                own = (1 - low) * width
                other = low * width
                at = 0 if first else own
                out[:, at : at + width] = bf16(total[:, own : own + width] + f32(mine[...]))
                if first:
                    out[:, width:] = jnp.zeros(mine.shape, jnp.bfloat16)
                else:
                    out[:, other : other + width] = bf16(
                        total[:, other : other + width] + f32(theirs[...])
                    )


def send_late_body(scalars, ins, outs, scratch):
    width = ins[0].shape[1] // 2

    @pl.when(scalars[1] == 1)
    def _():
        for out_ref in outs:
            for at, ref in enumerate(ins):
                out_ref[:, at * width : (at + 1) * width] = ref[:, :width]

    @pl.when(scalars[1] == 0)
    def _():
        for index in range(2 * len(ins)):
            out_ref, at = outs[index // len(ins)], index % len(ins)
            start = index % 2 * width
            out_ref[:, at * width : (at + 1) * width] = ins[index // 2][:, start : start + width]


def keep_late_body(scalars, ins, outs, scratch):
    one, two, prev, nxt, across = ins
    rows, own_cols, far_cols = outs
    width = one.shape[1]
    for first, (left, right, own, far) in ((1, (prev, nxt, one, across)), (0, (one, two, nxt, prev))):

        @pl.when(scalars[1] == first)
        def _(left=left, right=right, own=own, far=far):
            rows[:, :width] = left[...]
            rows[:, width:] = right[...]
            own_cols[...] = own[...]
            far_cols[...] = far[...]


def proj_body(scalars, ins, outs, scratch):
    outs[0][...] = bf16(ins[0][...] + f32(ins[1][...]))


def join_body(scalars, ins, outs, scratch):
    width = ins[0].shape[1]
    for at, ref in enumerate(ins):
        outs[0][:, at * width : (at + 1) * width] = ref[...]


def keep_body(width, scalars, ins, outs, scratch):
    proj, prev, nxt, across, far = ins
    rows, own_cols, far_cols = outs
    for first, (own, other, mine, theirs) in (
        (1, (proj, across, nxt, prev)),
        (0, (nxt, prev, proj, far)),
    ):

        @pl.when(scalars[1] == first)
        def _(own=own, other=other):
            own_cols[...] = own[...]
            far_cols[...] = other[...]

        for low, pair in ((1, (mine, theirs)), (0, (theirs, mine))):

            @pl.when((scalars[1] == first) & (scalars[2] == low))
            def _(pair=pair):
                for k in range(own_cols.shape[1] // width):
                    for at, ref in enumerate(pair):
                        start = (2 * k + at) * width
                        rows[:, start : start + width] = ref[:, k * width : (k + 1) * width]


def square_body(places, scalars, ins, outs, scratch):
    (cols,) = scratch
    rows = ins[: len(GROUPS)]
    for index, out_ref in enumerate(outs):
        for block, parts in enumerate(places):

            @pl.when(scalars[3 + index] == block)
            def _(parts=parts):
                width = cols.shape[1] // len(parts)
                for at, (which, start) in enumerate(parts):
                    cols[:, at * width : (at + 1) * width] = ins[which][:, start : start + width]

        start = 0
        for ref in rows:
            total = None
            for seq in range(ref.shape[0] // SEQ):
                tokens = pl.ds(seq * SEQ, SEQ)
                term = lax.dot_general(
                    ref[tokens, :],
                    cols[tokens, :],
                    (((0,), (0,)), ((), ())),
                    preferred_element_type=jnp.float32,
                )
                total = term * term if total is None else total + term * term
            out_ref[start : start + ref.shape[1], :] = bf16(total * (1.0 / 16384))
            start += ref.shape[1]


def cut_body(scalars, ins, outs, scratch):
    total = sum(f32(ref[...]) for ref in ins)
    height, width = outs[0].shape
    for index, out_ref in enumerate(outs):
        a, b = divmod(index, 2)
        out_ref[...] = bf16(total[a * height : (a + 1) * height, b * width : (b + 1) * width])


def last_body(scalars, ins, outs, scratch):
    half = outs[0].shape[0] // 2
    for odd in range(2):

        @pl.when(scalars[7] == odd)
        def _(odd=odd):
            for at in (0, half):
                total = None
                for index, ref in enumerate(ins):
                    start = at if index % 2 == odd else half - at
                    term = f32(ref[start : start + half, :])
                    total = term if total is None else total + term
                outs[0][at : at + half, :] = total


class Chain:
    def __init__(self, scalars):
        self.scalars = scalars
        self.token = jnp.zeros((8, 128), jnp.float32)

    def __call__(self, name, body, ins, outs, scratch=()):
        def kernel(scalars, token, *refs):
            in_refs, refs = refs[: len(ins)], refs[len(ins) :]
            out_refs, token_out, scratch_refs = refs[: len(outs)], refs[len(outs)], refs[len(outs) + 1 :]
            body(scalars, in_refs, out_refs, scratch_refs)
            token_out[...] = token[...]

        vmem = pl.BlockSpec(memory_space=pltpu.VMEM)
        *results, self.token = pl.pallas_call(
            kernel,
            out_shape=[*outs, like((8, 128), jnp.float32)],
            in_specs=[pl.BlockSpec(memory_space=pltpu.SMEM)] + [vmem] * (1 + len(ins)),
            out_specs=[vmem] * (len(outs) + 1),
            scratch_shapes=list(scratch),
            compiler_params=pltpu.CompilerParams(vmem_limit_bytes=VMEM_LIMIT),
            cost_estimate=pl.CostEstimate(flops=1, bytes_accessed=1, transcendentals=0),
            name=name,
        )(self.scalars, self.token, *ins)
        return results


VMEM_LIMIT = 16 * 1024 * 1024


def on_device(acts, grads, in_basis, out_basis):
    ex, tp = lax.axis_index("ex"), lax.axis_index("tp")
    x, z_lo, core = ex // (NZ_LO * NC), ex // NC % NZ_LO, ex % NC
    y, z_hi = tp // NZ_HI, tp % NZ_HI
    first = core == 0
    width = in_basis.shape[1]

    steps = (y + core - x + NX) % NX
    odd, turn = steps % 2, steps // 2
    blocks = [2 * (d ^ turn) + (goal ^ odd) for d in range(2) for goal in range(2)]
    scalars = jnp.stack([(y - x + NX) % NX, 1 - core, 1 - z_hi, *blocks, z_lo % 2])
    chain = Chain(scalars)

    with jax.named_scope("to_cores"):
        basis_in = move(jnp.where(first, out_basis, in_basis), other_core)
        own_basis = jnp.concatenate(
            [jnp.where(first, in_basis, basis_in), jnp.where(first, basis_in, out_basis)], axis=1
        )
        data_in = move(jnp.where(first, grads, acts), other_core)
        data = jnp.concatenate(
            [jnp.where(first, acts, data_in), jnp.where(first, data_in, grads)], axis=0
        )
    tokens, depth, double = data.shape[0], data.shape[1], own_basis.shape[1]
    near_of, far_of, zed_of, terms_of, half_of = {}, {}, {}, {}, {}
    sums_of, proj_of, sent_of, rows_of, cols_of = {}, {}, {}, {}, {}

    def zed(k, gated=True):
        own = chain("zed", copy_body, [own_basis], [like(own_basis.shape)])[0] if gated else own_basis
        zed_of[k] = move(own, lambda x, y, h, l, c: (x, y, h, l ^ k, c))

    def near(phase):
        own = own_basis
        if phase:
            (own,) = chain("near", copy_body, [zed_of[phase]], [like(own_basis.shape)])
        near_of[phase] = own, move(own, along_x(-1)), move(own, along_x(1))

    def far(phase):
        _, behind, before = near_of[phase]
        (own,) = chain("far", far_body, [before, behind], [like(own_basis.shape)])
        far_of[phase] = move(own, by_core_x)

    def project(phase, steps):
        own, behind, before = near_of[phase]
        return chain(
            "project",
            functools.partial(project_body, steps),
            [data, own, behind, far_of[phase], before],
            [like((tokens, double))] * len(steps),
            [pltpu.VMEM((depth, double), jnp.bfloat16)],
        )

    def two(phase):
        (term,) = project(phase, (2,))
        terms_of[phase] = [move(term, by_core_y)]

    def rest(phase):
        terms_of[phase] += project(phase, (1, 3, 0))

    def sums(phase):
        got, one, three, own = terms_of[phase]
        nxt, prv = chain("sums", sum_body, [one, three, got], [like((tokens, double))] * 2)
        sums_of[phase] = own, move(nxt, along_y(1)), move(prv, along_y(-1))

    def half(phase):
        shape = tokens, width
        sent, kept = chain("half", half_body, sums_of[phase], [like(shape), like(shape, jnp.float32)])
        half_of[phase] = kept, move(sent, other_half)

    def proj(phase):
        (proj_of[phase],) = chain("proj", proj_body, half_of[phase], [like((tokens, width))])

    def send(group):
        own = [proj_of[phase] for phase in GROUPS[group]]
        (own,) = chain("send", join_body, own, [like((tokens, width * len(own)))])
        prev = move(own, lambda x, y, h, l, c: (x, y + 1, h, l, 1) if c == 0 else (x, y, 1 - h, l, 0))
        nxt = move(own, lambda x, y, h, l, c: (x, y - 1, h, l, 1) if c == 0 else (x, y, h, l, 0))
        across = move(own, lambda x, y, h, l, c: (x, y + 2, h, l, 0) if c == 0 else None)
        swapped = move(prev, lambda x, y, h, l, c: (x, y, h, l, 1) if c == 0 else None)
        sent_of[group] = own, prev, nxt, across, swapped

    def take(group):
        own, prev, nxt, across, swapped = sent_of[group]
        nxt, across = chain("take", copy_body, [nxt, across], [like(own.shape)] * 2)
        sent_of[group] = own, prev, nxt, across, swapped

    def keep(group):
        shape = sent_of[group][0].shape
        rows_of[group], *cols_of[group] = chain(
            "keep",
            functools.partial(keep_body, width),
            sent_of[group],
            [like((tokens, 2 * shape[1])), like(shape), like(shape)],
        )

    def late(phase):
        total, away, kept = chain(
            "late",
            late_body,
            sums_of[phase],
            [like((tokens, double), jnp.float32)] + [like((tokens, width))] * 2,
        )
        mine = move(away, other_half)
        theirs = move(kept, lambda x, y, h, l, c: (x, y, 1 - h, l, c) if c else None)
        half_of[phase] = total, mine, theirs

    def full(phase):
        (proj_of[phase],) = chain("full", full_body, half_of[phase], [like((tokens, double))])

    def push(group):
        one, two = chain(
            "push",
            send_late_body,
            [proj_of[phase] for phase in GROUPS[group]],
            [like((tokens, width * len(GROUPS[group])))] * 2,
        )
        prev = move(one, lambda x, y, h, l, c: (x, y + 1, h, l, 1) if c == 0 else (x, y, h, l, 0))
        nxt = move(two, lambda x, y, h, l, c: (x, y - 1, h, l, 1) if c == 0 else (x, y, h, l, 0))
        across = move(one, lambda x, y, h, l, c: (x, y + 2, h, l, 0) if c == 0 else None)
        sent_of[group] = one, two, prev, nxt, across

    def hold(group):
        shape = sent_of[group][0].shape
        rows_of[group], *cols_of[group] = chain(
            "hold", keep_late_body, sent_of[group], [like((tokens, 2 * shape[1])), like(shape), like(shape)]
        )

    run = dict(
        late=late, take=take, full=full, push=push, hold=hold,
        zed=zed, near=near, far=far, two=two, rest=rest, sum=sums, half=half, proj=proj, send=send, keep=keep
    )
    near(0)
    for k in EARLY:
        zed(k, gated=False)
    for item in ORDER:
        with jax.named_scope(item[:-1]):
            run[item[:-1]](int(item[-1]))

    height = NZ_LO * width
    with jax.named_scope("squares"):
        rows = [rows_of[group] for group in range(len(GROUPS))]
        cols = [cols for group in range(len(GROUPS)) for cols in cols_of[group]]
        places = []
        for block in range(2):
            for part in range(2):
                found = []
                for k in (2 * part, 2 * part + 1):
                    group = next(at for at, members in enumerate(GROUPS) if k in members)
                    found.append((len(rows) + 2 * group + block, GROUPS[group].index(k) * width))
                places.append(found)
        tiles = chain(
            "squares",
            functools.partial(square_body, places),
            rows + cols,
            [like((2 * height, double))] * 4,
            [pltpu.VMEM((tokens, double), jnp.bfloat16)],
        )
    with jax.named_scope("sum_along_x"):
        arrived = []
        for d in (1, 0):
            for goal in range(2):

                def target(x, y, h, l, c, d=d, goal=goal):
                    odd = (y + c - x) % 2
                    return x + odd + 2 * d, y, h, l, goal ^ odd

                arrived.append(move(tiles[2 * d + goal], target))
        parts = chain("cut", cut_body, arrived, [like((height, width))] * 4)
    with jax.named_scope("sum_along_z"):
        got = [
            move(
                parts[2 * a + b],
                lambda x, y, h, l, c, a=a, b=b: (x, y, a ^ (l >> 1), l ^ (2 * c + b), h),
            )
            for a in range(2)
            for b in range(2)
        ]
        (result,) = chain("last", last_body, got, [like((height, width), jnp.float32)])
    return result


def solution(mesh):
    return jax.shard_map(
        on_device,
        mesh=mesh,
        in_specs=(P("ex", "tp"), P("ex", "tp"), P("tp", "ex"), P("tp", "ex")),
        out_specs=P("tp", "ex"),
        check_vma=False,
    )
```

```python
import functools

import jax
import jax.numpy as jnp
from jax import lax
from jax.experimental import pallas as pl
from jax.experimental.pallas import tpu as pltpu
from jax.sharding import PartitionSpec as P

SEQ = 256
NX, NY, NZ_LO, NZ_HI, NC = 4, 4, 4, 2, 2
EARLY = (1, 2)
GROUPS = ((0, 1), (2, 3))
ORDER = (
    "far0", "near1", "two0", "rest0", "zed3", "far1", "near2", "sum0", "two1", "rest1", "far2",
    "near3", "half0", "sum1", "two2", "rest2", "far3", "sum2", "half1", "two3", "rest3", "proj0",
    "sum3", "late2", "proj1", "send0", "late3", "full2", "full3", "keep0", "push1", "hold1",
)


def position(index):
    ex, tp = divmod(index, NY * NZ_HI)
    x, rest = divmod(ex, NZ_LO * NC)
    z_lo, core = divmod(rest, NC)
    y, z_hi = divmod(tp, NZ_HI)
    return x, y, z_hi, z_lo, core


def number(x, y, z_hi, z_lo, core):
    ex = ((x % NX) * NZ_LO + z_lo) * NC + core
    return ex * NY * NZ_HI + (y % NY) * NZ_HI + z_hi


def move(array, target):
    pairs = []
    for index in range(NX * NY * NZ_LO * NZ_HI * NC):
        goal = target(*position(index))
        if goal is not None:
            pairs.append((index, number(*goal)))
    return lax.ppermute(array, ("ex", "tp"), pairs)


def other_core(x, y, h, l, c):
    return x, y, h, l, 1 - c


def along_x(step):
    return lambda x, y, h, l, c: (x + step, y, h, l, c)


def along_y(step):
    return lambda x, y, h, l, c: (x, y + step, h, l, c)


def by_core_x(x, y, h, l, c):
    return x + 1 - 2 * c, y, h, l, c


def by_core_y(x, y, h, l, c):
    return x, y + 1 - 2 * c, h, l, c


def other_half(x, y, h, l, c):
    return x, y, 1 - h, l, c


def f32(value):
    return value.astype(jnp.float32)


def bf16(value):
    return value.astype(jnp.bfloat16)


def like(shape, dtype=jnp.bfloat16):
    return jax.ShapeDtypeStruct(shape, dtype)


def pick(out_ref, refs, index):
    for at, ref in enumerate(refs):

        @pl.when(index == at)
        def _(ref=ref):
            out_ref[...] = ref[...]


def copy_body(scalars, ins, outs, scratch):
    for in_ref, out_ref in zip(ins, outs):
        out_ref[...] = in_ref[...]


def far_body(scalars, ins, outs, scratch):
    pick(outs[0], ins, 1 - scalars[1])


def project_body(steps, scalars, ins, outs, scratch):
    data, *pieces = ins
    (basis,) = scratch
    for step, out_ref in zip(steps, outs):
        pick(basis, pieces, lax.rem(scalars[0] + step, NX))
        out_ref[...] = bf16(jnp.dot(data[...], basis[...], preferred_element_type=jnp.float32))


def sum_body(scalars, ins, outs, scratch):
    one, three, got = ins
    nxt, prv = outs

    @pl.when(scalars[1] == 1)
    def _():
        nxt[...] = bf16(f32(one[...]) + f32(got[...]))
        prv[...] = three[...]

    @pl.when(scalars[1] == 0)
    def _():
        nxt[...] = one[...]
        prv[...] = bf16(f32(three[...]) + f32(got[...]))


def half_body(scalars, ins, outs, scratch):
    sent, kept = outs
    width = sent.shape[1]
    for low, (keep, send) in ((1, (0, width)), (0, (width, 0))):

        @pl.when(scalars[2] == low)
        def _(keep=keep, send=send):
            sent[...] = bf16(sum(f32(ref[:, send : send + width]) for ref in ins))
            kept[...] = sum(f32(ref[:, keep : keep + width]) for ref in ins)


def late_body(scalars, ins, outs, scratch):
    total_ref, away, kept = outs
    width = away.shape[1]
    total = sum(f32(ref[...]) for ref in ins)
    total_ref[...] = total
    for low, (keep, send) in ((1, (0, width)), (0, (width, 0))):

        @pl.when(scalars[2] == low)
        def _(keep=keep, send=send):
            away[...] = bf16(total[:, send : send + width])
            kept[...] = bf16(total[:, keep : keep + width])


def full_body(scalars, ins, outs, scratch):
    total, mine, theirs = ins
    (out,) = outs
    width = mine.shape[1]
    for first in (1, 0):
        for low in (1, 0):

            @pl.when((scalars[1] == first) & (scalars[2] == low))
            def _(first=first, low=low):
                own = (1 - low) * width
                other = low * width
                at = 0 if first else own
                out[:, at : at + width] = bf16(total[:, own : own + width] + f32(mine[...]))
                if first:
                    out[:, width:] = jnp.zeros(mine.shape, jnp.bfloat16)
                else:
                    out[:, other : other + width] = bf16(
                        total[:, other : other + width] + f32(theirs[...])
                    )


def send_late_body(scalars, ins, outs, scratch):
    width = ins[0].shape[1] // 2

    @pl.when(scalars[1] == 1)
    def _():
        for out_ref in outs:
            for at, ref in enumerate(ins):
                out_ref[:, at * width : (at + 1) * width] = ref[:, :width]

    @pl.when(scalars[1] == 0)
    def _():
        for index in range(2 * len(ins)):
            out_ref, at = outs[index // len(ins)], index % len(ins)
            start = index % 2 * width
            out_ref[:, at * width : (at + 1) * width] = ins[index // 2][:, start : start + width]


def keep_late_body(scalars, ins, outs, scratch):
    one, two, prev, nxt, across = ins
    rows, own_cols, far_cols = outs
    width = one.shape[1]
    for first, (left, right, own, far) in ((1, (prev, nxt, one, across)), (0, (one, two, nxt, prev))):

        @pl.when(scalars[1] == first)
        def _(left=left, right=right, own=own, far=far):
            rows[:, :width] = left[...]
            rows[:, width:] = right[...]
            own_cols[...] = own[...]
            far_cols[...] = far[...]


def proj_body(scalars, ins, outs, scratch):
    outs[0][...] = bf16(ins[0][...] + f32(ins[1][...]))


def join_body(scalars, ins, outs, scratch):
    width = ins[0].shape[1]
    for at, ref in enumerate(ins):
        outs[0][:, at * width : (at + 1) * width] = ref[...]


def keep_body(width, scalars, ins, outs, scratch):
    proj, prev, nxt, across, far = ins
    rows, own_cols, far_cols = outs
    for first, (own, other, mine, theirs) in (
        (1, (proj, across, nxt, prev)),
        (0, (nxt, prev, proj, far)),
    ):

        @pl.when(scalars[1] == first)
        def _(own=own, other=other):
            own_cols[...] = own[...]
            far_cols[...] = other[...]

        for low, pair in ((1, (mine, theirs)), (0, (theirs, mine))):

            @pl.when((scalars[1] == first) & (scalars[2] == low))
            def _(pair=pair):
                for k in range(own_cols.shape[1] // width):
                    for at, ref in enumerate(pair):
                        start = (2 * k + at) * width
                        rows[:, start : start + width] = ref[:, k * width : (k + 1) * width]


def square_body(places, scalars, ins, outs, scratch):
    (cols,) = scratch
    rows = ins[: len(GROUPS)]
    for index, out_ref in enumerate(outs):
        for block, parts in enumerate(places):

            @pl.when(scalars[3 + index] == block)
            def _(parts=parts):
                width = cols.shape[1] // len(parts)
                for at, (which, start) in enumerate(parts):
                    cols[:, at * width : (at + 1) * width] = ins[which][:, start : start + width]

        start = 0
        for ref in rows:
            total = None
            for seq in range(ref.shape[0] // SEQ):
                tokens = pl.ds(seq * SEQ, SEQ)
                term = lax.dot_general(
                    ref[tokens, :],
                    cols[tokens, :],
                    (((0,), (0,)), ((), ())),
                    preferred_element_type=jnp.float32,
                )
                total = term * term if total is None else total + term * term
            out_ref[start : start + ref.shape[1], :] = bf16(total * (1.0 / 16384))
            start += ref.shape[1]


def cut_body(scalars, ins, outs, scratch):
    total = sum(f32(ref[...]) for ref in ins)
    height, width = outs[0].shape
    for index, out_ref in enumerate(outs):
        a, b = divmod(index, 2)
        out_ref[...] = bf16(total[a * height : (a + 1) * height, b * width : (b + 1) * width])


def last_body(scalars, ins, outs, scratch):
    half = outs[0].shape[0] // 2
    for odd in range(2):

        @pl.when(scalars[7] == odd)
        def _(odd=odd):
            for at in (0, half):
                total = None
                for index, ref in enumerate(ins):
                    start = at if index % 2 == odd else half - at
                    term = f32(ref[start : start + half, :])
                    total = term if total is None else total + term
                outs[0][at : at + half, :] = total


class Chain:
    def __init__(self, scalars):
        self.scalars = scalars
        self.token = jnp.zeros((8, 128), jnp.float32)

    def __call__(self, name, body, ins, outs, scratch=()):
        def kernel(scalars, token, *refs):
            in_refs, refs = refs[: len(ins)], refs[len(ins) :]
            out_refs, token_out, scratch_refs = refs[: len(outs)], refs[len(outs)], refs[len(outs) + 1 :]
            body(scalars, in_refs, out_refs, scratch_refs)
            token_out[...] = token[...]

        vmem = pl.BlockSpec(memory_space=pltpu.VMEM)
        *results, self.token = pl.pallas_call(
            kernel,
            out_shape=[*outs, like((8, 128), jnp.float32)],
            in_specs=[pl.BlockSpec(memory_space=pltpu.SMEM)] + [vmem] * (1 + len(ins)),
            out_specs=[vmem] * (len(outs) + 1),
            scratch_shapes=list(scratch),
            compiler_params=pltpu.CompilerParams(vmem_limit_bytes=VMEM_LIMIT),
            cost_estimate=pl.CostEstimate(flops=1, bytes_accessed=1, transcendentals=0),
            name=name,
        )(self.scalars, self.token, *ins)
        return results


VMEM_LIMIT = 16 * 1024 * 1024


def on_device(acts, grads, in_basis, out_basis):
    ex, tp = lax.axis_index("ex"), lax.axis_index("tp")
    x, z_lo, core = ex // (NZ_LO * NC), ex // NC % NZ_LO, ex % NC
    y, z_hi = tp // NZ_HI, tp % NZ_HI
    first = core == 0
    width = in_basis.shape[1]

    steps = (y + core - x + NX) % NX
    odd, turn = steps % 2, steps // 2
    blocks = [2 * (d ^ turn) + (goal ^ odd) for d in range(2) for goal in range(2)]
    scalars = jnp.stack([(y - x + NX) % NX, 1 - core, 1 - z_hi, *blocks, z_lo % 2])
    chain = Chain(scalars)

    with jax.named_scope("to_cores"):
        basis_in = move(jnp.where(first, out_basis, in_basis), other_core)
        own_basis = jnp.concatenate(
            [jnp.where(first, in_basis, basis_in), jnp.where(first, basis_in, out_basis)], axis=1
        )
        data_in = move(jnp.where(first, grads, acts), other_core)
        data = jnp.concatenate(
            [jnp.where(first, acts, data_in), jnp.where(first, data_in, grads)], axis=0
        )
    tokens, depth, double = data.shape[0], data.shape[1], own_basis.shape[1]
    near_of, far_of, zed_of, terms_of, half_of = {}, {}, {}, {}, {}
    sums_of, proj_of, sent_of, rows_of, cols_of = {}, {}, {}, {}, {}

    def zed(k, gated=True):
        own = chain("zed", copy_body, [own_basis], [like(own_basis.shape)])[0] if gated else own_basis
        zed_of[k] = move(own, lambda x, y, h, l, c: (x, y, h, l ^ k, c))

    def near(phase):
        own = own_basis
        if phase:
            (own,) = chain("near", copy_body, [zed_of[phase]], [like(own_basis.shape)])
        near_of[phase] = own, move(own, along_x(-1)), move(own, along_x(1))

    def far(phase):
        _, behind, before = near_of[phase]
        (own,) = chain("far", far_body, [before, behind], [like(own_basis.shape)])
        far_of[phase] = move(own, by_core_x)

    def project(phase, steps):
        own, behind, before = near_of[phase]
        return chain(
            "project",
            functools.partial(project_body, steps),
            [data, own, behind, far_of[phase], before],
            [like((tokens, double))] * len(steps),
            [pltpu.VMEM((depth, double), jnp.bfloat16)],
        )

    def two(phase):
        (term,) = project(phase, (2,))
        terms_of[phase] = [move(term, by_core_y)]

    def rest(phase):
        terms_of[phase] += project(phase, (1, 3, 0))

    def sums(phase):
        got, one, three, own = terms_of[phase]
        nxt, prv = chain("sums", sum_body, [one, three, got], [like((tokens, double))] * 2)
        sums_of[phase] = own, move(nxt, along_y(1)), move(prv, along_y(-1))

    def half(phase):
        shape = tokens, width
        sent, kept = chain("half", half_body, sums_of[phase], [like(shape), like(shape, jnp.float32)])
        half_of[phase] = kept, move(sent, other_half)

    def proj(phase):
        (proj_of[phase],) = chain("proj", proj_body, half_of[phase], [like((tokens, width))])

    def send(group):
        own = [proj_of[phase] for phase in GROUPS[group]]
        (own,) = chain("send", join_body, own, [like((tokens, width * len(own)))])
        prev = move(own, lambda x, y, h, l, c: (x, y + 1, h, l, 1) if c == 0 else (x, y, 1 - h, l, 0))
        nxt = move(own, lambda x, y, h, l, c: (x, y - 1, h, l, 1) if c == 0 else (x, y, h, l, 0))
        across = move(own, lambda x, y, h, l, c: (x, y + 2, h, l, 0) if c == 0 else None)
        swapped = move(prev, lambda x, y, h, l, c: (x, y, h, l, 1) if c == 0 else None)
        sent_of[group] = own, prev, nxt, across, swapped

    def keep(group):
        shape = sent_of[group][0].shape
        rows_of[group], *cols_of[group] = chain(
            "keep",
            functools.partial(keep_body, width),
            sent_of[group],
            [like((tokens, 2 * shape[1])), like(shape), like(shape)],
        )

    def late(phase):
        total, away, kept = chain(
            "late",
            late_body,
            sums_of[phase],
            [like((tokens, double), jnp.float32)] + [like((tokens, width))] * 2,
        )
        mine = move(away, other_half)
        theirs = move(kept, lambda x, y, h, l, c: (x, y, 1 - h, l, c) if c else None)
        half_of[phase] = total, mine, theirs

    def full(phase):
        (proj_of[phase],) = chain("full", full_body, half_of[phase], [like((tokens, double))])

    def push(group):
        one, two = chain(
            "push",
            send_late_body,
            [proj_of[phase] for phase in GROUPS[group]],
            [like((tokens, width * len(GROUPS[group])))] * 2,
        )
        prev = move(one, lambda x, y, h, l, c: (x, y + 1, h, l, 1) if c == 0 else (x, y, h, l, 0))
        nxt = move(two, lambda x, y, h, l, c: (x, y - 1, h, l, 1) if c == 0 else (x, y, h, l, 0))
        across = move(one, lambda x, y, h, l, c: (x, y + 2, h, l, 0) if c == 0 else None)
        sent_of[group] = one, two, prev, nxt, across

    def hold(group):
        shape = sent_of[group][0].shape
        rows_of[group], *cols_of[group] = chain(
            "hold", keep_late_body, sent_of[group], [like((tokens, 2 * shape[1])), like(shape), like(shape)]
        )

    run = dict(
        late=late, full=full, push=push, hold=hold,
        zed=zed, near=near, far=far, two=two, rest=rest, sum=sums, half=half, proj=proj, send=send, keep=keep
    )
    near(0)
    for k in EARLY:
        zed(k, gated=False)
    for item in ORDER:
        with jax.named_scope(item[:-1]):
            run[item[:-1]](int(item[-1]))

    height = NZ_LO * width
    with jax.named_scope("squares"):
        rows = [rows_of[group] for group in range(len(GROUPS))]
        cols = [cols for group in range(len(GROUPS)) for cols in cols_of[group]]
        places = []
        for block in range(2):
            for part in range(2):
                found = []
                for k in (2 * part, 2 * part + 1):
                    group = next(at for at, members in enumerate(GROUPS) if k in members)
                    found.append((len(rows) + 2 * group + block, GROUPS[group].index(k) * width))
                places.append(found)
        tiles = chain(
            "squares",
            functools.partial(square_body, places),
            rows + cols,
            [like((2 * height, double))] * 4,
            [pltpu.VMEM((tokens, double), jnp.bfloat16)],
        )
    with jax.named_scope("sum_along_x"):
        arrived = []
        for d in (1, 0):
            for goal in range(2):

                def target(x, y, h, l, c, d=d, goal=goal):
                    odd = (y + c - x) % 2
                    return x + odd + 2 * d, y, h, l, goal ^ odd

                arrived.append(move(tiles[2 * d + goal], target))
        parts = chain("cut", cut_body, arrived, [like((height, width))] * 4)
    with jax.named_scope("sum_along_z"):
        got = [
            move(
                parts[2 * a + b],
                lambda x, y, h, l, c, a=a, b=b: (x, y, a ^ (l >> 1), l ^ (2 * c + b), h),
            )
            for a in range(2)
            for b in range(2)
        ]
        (result,) = chain("last", last_body, got, [like((height, width), jnp.float32)])
    return result


def solution(mesh):
    return jax.shard_map(
        on_device,
        mesh=mesh,
        in_specs=(P("ex", "tp"), P("ex", "tp"), P("tp", "ex"), P("tp", "ex")),
        out_specs=P("tp", "ex"),
        check_vma=False,
    )
```
